32 devices in a mesh: bed: 8 (over y, x, core), layer: 4 (over z).
Axes of the slice: x: 2, y: 2, z: 4, core: 2. Of those that a mesh axis runs over, the one named last changes fastest.
Arguments:
- concentration: float32 [8, 1024, 4096], P('layer', 'bed'), may hold values from 0.2 to 2
- east_velocity: bfloat16 [8, 1024, 4096], P('layer', 'bed'), may hold values from -3 to 3
- north_velocity: bfloat16 [8, 1024, 4096], P('layer', 'bed'), may hold values from -3 to 3
- settling: float32 [1024, 4096], P('bed'), may hold values from 0.02 to 0.15
- surface: float32 [1024, 4096], P('bed'), may hold values from 1.8 to 6
- bed_level: float32 [1024, 4096], P('bed'), may hold values from -1 to 1
- erosion: float32 [1024, 4096], P('bed'), may hold values from 0 to 0.08
- wet_mask: int32 [1024, 4096], P('bed'), may hold values 0 or 1
Outputs:
- new_concentration: float32 [8, 1024, 4096], P('layer', 'bed')
- new_bed: float32 [1024, 4096], P('bed')
The draws below stay inside these ranges and needn't reach their ends.
Inputs may be any that keep to these rules, and one draw needn't show every extreme that they name: `wet_mask`: 1 marks a wet cell, 0 a dry one.
All inputs are finite; a program needn't handle non-finite values. No bound on the sum of `wet_mask` on one device may be relied on, other than what follows from the above.
Results may differ from the reference program's by a relative error of at most 0.0003.
Values sent between devices are 32-bit elements; how exact they have to be, the bound alone decides.
A program may use at most 128 MiB of HBM per device.

```python
import math
import jax
import jax.numpy as jnp
from jax import lax

NY = 4096
SWEEPS = 4
NX = 1024
LAYERS = 8


def set_ends(entries, own_key, low, high):
    spot = [jax.random.randint(jax.random.fold_in(own_key, axis), (), 0, length) for axis, length in enumerate(entries.shape)]
    main_axis = entries.shape.index(max(entries.shape))
    next_to = spot[:main_axis] + [(spot[main_axis] + 1) % entries.shape[main_axis]] + spot[main_axis + 1:]
    return entries.at[tuple(spot)].set(low).at[tuple(next_to)].set(high)


def block_scale(stream_key, dims, shards, low, largest):
    level = 1.0
    for dim, parts in shards:
        draws = jax.random.uniform(jax.random.fold_in(jax.random.fold_in(stream_key, 6), dim), (parts,), jnp.float32, low / len(shards), largest / len(shards))
        level = level * jnp.repeat(jnp.exp(draws), dims[dim] // parts).reshape((-1,) + (1,) * (len(dims) - 1 - dim))
    return level


def gaussian(rng, dims, deviation, bound, pieces=(), held_as=jnp.bfloat16):
    result = deviation * jax.random.normal(rng, dims, jnp.float32)
    if pieces:
        result = result * block_scale(rng, dims, pieces, -0.22, 0.18)
    return jnp.clip(result, -bound, bound).astype(held_as)


def setup_inputs(seed: int = 0) -> dict:
    seeds = jax.random.split(jax.random.key(seed), 9)
    return {
        "concentration": jnp.clip(0.2 + 1.8 * jax.random.uniform(seeds[0], (LAYERS, NX, NY), jnp.float32) ** block_scale(seeds[0], (LAYERS, NX, NY), ((0, 4), (1, 8)), -0.2, 0.2), 0.2, 2.0),
        "east_velocity": gaussian(seeds[1], (LAYERS, NX, NY), 1.0, 3.0, ((0, 4), (1, 8))),
        "north_velocity": gaussian(seeds[2], (LAYERS, NX, NY), 1.0, 3.0, ((0, 4), (1, 8))),
        "settling": jnp.clip(jnp.exp(math.log(0.15) - 2.014903 * jax.random.uniform(seeds[3], (NX, NY), jnp.float32) ** block_scale(seeds[3], (NX, NY), ((0, 8),), -0.2, 0.2)), 0.02, 0.15),
        "surface": jnp.clip(1.8 + 4.2 * jax.random.uniform(seeds[4], (NX, NY), jnp.float32) ** block_scale(seeds[4], (NX, NY), ((0, 8),), -0.2, 0.2), 1.8, 6.0),
        "bed_level": jnp.clip(jax.random.uniform(seeds[5], (NX, NY), jnp.float32, -1.0, 1.0) * block_scale(seeds[5], (NX, NY), ((0, 8),), -0.4, 0.0), -1.0, 1.0),
        "erosion": jnp.clip(0.08 * jax.random.uniform(seeds[6], (NX, NY), jnp.float32) ** block_scale(seeds[6], (NX, NY), ((0, 8),), -0.2, 0.2), 0.0, 0.08),
        "wet_mask": set_ends((jax.random.randint(seeds[7], (NX, NY), 0, 8) < 7).astype(jnp.int32), jax.random.fold_in(seeds[7], 1), 0, 1),
    }


ADVECT_RATE = 0.1
FLUX_GAIN = 0.15
POROSITY_GAIN = 1.0 / 0.6
RELAX_RATE = 0.2
CRIT_SLOPE = 0.5
DEPTH_FLOOR = 1.0


def face_divergence(values, speeds, which_axis):
    length_here = values.shape[which_axis]
    left_val = lax.slice_in_dim(values, 0, length_here - 1, axis=which_axis)
    right_val = lax.slice_in_dim(values, 1, length_here, axis=which_axis)
    left_spd = lax.slice_in_dim(speeds, 0, length_here - 1, axis=which_axis)
    right_spd = lax.slice_in_dim(speeds, 1, length_here, axis=which_axis)
    face_speed = 0.5 * (left_spd + right_spd)
    face_flux = jnp.maximum(face_speed, 0.0) * left_val + jnp.minimum(face_speed, 0.0) * right_val
    return lax.slice_in_dim(face_flux, 1, length_here - 1, axis=which_axis) - lax.slice_in_dim(face_flux, 0, length_here - 2, axis=which_axis)


def slide_sweep(height, wetness):
    drop_x = height[:-1, :] - height[1:, :]
    move_x = RELAX_RATE * (drop_x - jnp.clip(drop_x, -CRIT_SLOPE, CRIT_SLOPE)) * wetness[:-1, :] * wetness[1:, :]
    drop_y = height[:, :-1] - height[:, 1:]
    move_y = RELAX_RATE * (drop_y - jnp.clip(drop_y, -CRIT_SLOPE, CRIT_SLOPE)) * wetness[:, :-1] * wetness[:, 1:]
    return height[1:-1, 1:-1] - move_x[1:, 1:-1] + move_x[:-1, 1:-1] - move_y[1:-1, 1:] + move_y[1:-1, :-1]


def reference(concentration, east_velocity, north_velocity, settling, surface, bed_level, erosion, wet_mask):
    water_depth = surface - bed_level
    layer_thick = water_depth / LAYERS
    wet_float = wet_mask.astype(jnp.float32)

    def one_layer(summed, layer_pos):
        here = concentration[layer_pos]
        above_flag = (layer_pos + 1 < LAYERS).astype(jnp.float32)
        upper = concentration[jnp.minimum(layer_pos + 1, LAYERS - 1)] * above_flag
        bottom_flag = (layer_pos == 0).astype(jnp.float32)
        east_speed = east_velocity[layer_pos].astype(jnp.float32)
        north_speed = north_velocity[layer_pos].astype(jnp.float32)
        pad_x = ((1, 1), (0, 0))
        pad_y = ((0, 0), (1, 1))
        advect = face_divergence(jnp.pad(here, pad_x), jnp.pad(east_speed, pad_x), 0) + face_divergence(jnp.pad(here, pad_y), jnp.pad(north_speed, pad_y), 1)
        source = settling * upper - settling * here + bottom_flag * erosion
        settled = here - ADVECT_RATE * advect + (LAYERS / water_depth) * source
        east_wide = jnp.pad(east_speed * here * layer_thick, pad_x)
        north_wide = jnp.pad(north_speed * here * layer_thick, pad_y)
        spread = 0.5 * (east_wide[2:, :] - east_wide[:-2, :] + north_wide[:, 2:] - north_wide[:, :-2])
        return summed + FLUX_GAIN * spread - bottom_flag * settling * here, settled

    summed, settled = lax.scan(one_layer, jnp.zeros(bed_level.shape, jnp.float32), jnp.arange(LAYERS, dtype=jnp.int32))
    height = bed_level - POROSITY_GAIN * wet_float * (summed + erosion)
    wet_wide = jnp.pad(wet_float, 1)
    for sweep_index in range(SWEEPS):
        height = slide_sweep(jnp.pad(height, 1), wet_wide)
    new_depth = jnp.maximum(surface - height, DEPTH_FLOOR)
    return settled * (water_depth / new_depth), height
```

```python
import functools

import jax
import jax.numpy as jnp
from jax import lax
from jax.experimental import pallas as pl
from jax.experimental.pallas import tpu as pltpu
from jax.sharding import PartitionSpec as P

SWEEPS = 4
ADVECT_RATE = 0.1
FLUX_GAIN = 0.15
POROSITY_GAIN = 1.0 / 0.6
RELAX_RATE = 0.2
CRIT_SLOPE = 0.5
DEPTH_FLOOR = 1.0

CH = 16
PAD = 8
SLOTS = 4
LAG = 1
MESH = pl.DeviceIdType.MESH


def down_rows(x, first):
    row = lax.broadcasted_iota(jnp.int32, x.shape, 0)
    return jnp.where(row == 0, first, pltpu.roll(x, 1, 0))


def up_rows(x, last):
    n = x.shape[0]
    row = lax.broadcasted_iota(jnp.int32, x.shape, 0)
    return jnp.where(row == n - 1, last, pltpu.roll(x, n - 1, 0))


def from_left(x):
    col = lax.broadcasted_iota(jnp.int32, x.shape, 1)
    return jnp.where(col == 0, 0.0, pltpu.roll(x, 1, 1))


def from_right(x):
    w = x.shape[1]
    col = lax.broadcasted_iota(jnp.int32, x.shape, 1)
    return jnp.where(col == w - 1, 0.0, pltpu.roll(x, w - 1, 1))


def face(speed_a, speed_b, val_a, val_b):
    f = 0.5 * (speed_a + speed_b)
    return jnp.maximum(f, 0.0) * val_a + jnp.minimum(f, 0.0) * val_b


def move(drop, wet_a, wet_b):
    return RELAX_RATE * (drop - jnp.clip(drop, -CRIT_SLOPE, CRIT_SLOPE)) * wet_a * wet_b


def kernel(
    nb, nl, c_hbm, u_hbm, v_hbm, sett_hbm, surf_hbm, bed_hbm, eros_hbm, wet_hbm,
    out, out_h,
    cs, us, vs, es, ws, ce, ue, we, sett, surf, bed, wetp, ha, hb, dbuf, ubuf, cup,
    edge_out, halo, prv, nxt,
    ring_sem, edge_sem, full_sem, halo_ss, halo_rs, wet_ss, wet_rs, h_ss, h_rs,
    d_ss, d_rs, u_ss, u_rs, c_ss, c_rs,
):
    lh, rows, width = c_hbm.shape
    n = rows // CH
    layers = lh * nl
    l = lax.axis_index("layer")
    b = lax.axis_index("bed")
    has_dn, has_up = l > 0, l < nl - 1
    has_lo, has_hi = b > 0, b < nb - 1
    bottom = (l == 0).astype(jnp.float32)
    neighbours = (
        (has_lo, (b - 1, l)), (has_hi, (b + 1, l)), (has_dn, (b, l - 1)), (has_up, (b, l + 1)),
    )

    def ds(k, size=CH, off=0):
        return pl.ds(pl.multiple_of(k * CH + off, 8), size)

    edges = []
    for side, (start8, start16) in enumerate(((0, 0), (rows - 8, rows - 16))):
        edges.append((
            pltpu.make_async_copy(c_hbm.at[:, pl.ds(start8, 8)], ce.at[side], edge_sem.at[side, 0]),
            pltpu.make_async_copy(u_hbm.at[:, pl.ds(start16, 16)], ue.at[side], edge_sem.at[side, 1]),
            pltpu.make_async_copy(wet_hbm.at[pl.ds(start8, 8)], we.at[side], edge_sem.at[side, 2]),
        ))
    fulls = [
        pltpu.make_async_copy(src, dst, full_sem.at[i])
        for i, (src, dst) in enumerate(((surf_hbm, surf), (bed_hbm, bed), (sett_hbm, sett)))
    ]

    def ring(k):
        s = lax.rem(k, SLOTS)
        return (
            pltpu.make_async_copy(c_hbm.at[:, ds(k)], cs.at[s], ring_sem.at[s, 0]),
            pltpu.make_async_copy(u_hbm.at[:, ds(k)], us.at[s], ring_sem.at[s, 1]),
            pltpu.make_async_copy(v_hbm.at[:, ds(k)], vs.at[s], ring_sem.at[s, 2]),
            pltpu.make_async_copy(eros_hbm.at[ds(k)], es.at[s], ring_sem.at[s, 3]),
            pltpu.make_async_copy(wet_hbm.at[ds(k)], ws.at[s], ring_sem.at[s, 4]),
        )

    for group in edges:
        for copy in group:
            copy.start()
    for copy in fulls:
        copy.start()
    for k in range(min(SLOTS - 1, n)):
        for copy in ring(k):
            copy.start()

    def remote(src, dst, ss, rs, target):
        return pltpu.make_async_remote_copy(
            src_ref=src, dst_ref=dst, send_sem=ss, recv_sem=rs, device_id=target,
            device_id_type=MESH,
        )

    def halo_copy(side):
        return remote(
            edge_out.at[side], halo.at[1 - side], halo_ss.at[side], halo_rs.at[1 - side],
            (b - 1 + 2 * side, l),
        )

    pad_src = (PAD, rows)
    pad_dst = (PAD + rows, 0)

    def wet_copy(side):
        return remote(
            wetp.at[pl.ds(pad_src[side], PAD)], wetp.at[pl.ds(pad_dst[side], PAD)],
            wet_ss.at[side], wet_rs.at[1 - side], (b - 1 + 2 * side, l),
        )

    def height_copy(side):
        return remote(
            ha.at[pl.ds(pad_src[side], PAD)], ha.at[pl.ds(pad_dst[side], PAD)],
            h_ss.at[side], h_rs.at[1 - side], (b - 1 + 2 * side, l),
        )

    def sum_down(k):
        return remote(dbuf.at[ds(k)], dbuf.at[ds(k)], d_ss.at[k], d_rs.at[k], (b, l - 1))

    def sum_up(k):
        return remote(ubuf.at[ds(k)], ubuf.at[ds(k)], u_ss.at[k], u_rs.at[k], (b, l + 1))

    def conc_down(k):
        return remote(c_hbm.at[0, ds(k)], cup.at[ds(k)], c_ss.at[k], c_rs.at[k], (b, l - 1))

    present = (has_lo, has_hi)

    barrier = pltpu.get_barrier_semaphore()
    for there, target in neighbours:
        @pl.when(there)
        def _():
            pl.semaphore_signal(barrier, inc=1, device_id=target, device_id_type=MESH)
    pl.semaphore_wait(barrier, sum(there.astype(jnp.int32) for there, _ in neighbours))

    def start_conc(k):
        @pl.when(has_dn & (k < n))
        def _():
            conc_down(k).start()

    ahead = nl - 1 - l

    start_conc(jnp.int32(0))

    for copy in fulls:
        copy.wait()
    for side in range(2):
        for copy in edges[side]:
            copy.wait()
        row8, row16, row = ((0, 0, 0), (7, 15, rows - 1))[side]
        thick = (surf[row:row + 1, :] - bed[row:row + 1, :]) / layers
        for m in range(lh):
            c = ce[side, m, row8:row8 + 1, :]
            u = ue[side, m].astype(jnp.float32)[row16:row16 + 1, :]
            edge_out[side, m:m + 1, :] = c
            edge_out[side, lh + m:lh + m + 1, :] = u
            edge_out[side, 2 * lh + m:2 * lh + m + 1, :] = u * c * thick
        for row in range(3 * lh, 8):
            edge_out[side, row:row + 1, :] = jnp.zeros((1, width), jnp.float32)
        wetp[pl.ds(pad_src[side], PAD), :] = we[side].astype(jnp.float32)

        @pl.when(present[side])
        def _():
            halo_copy(side).start()
            wet_copy(side).start()

        @pl.when(jnp.logical_not(present[side]))
        def _():
            zeros = jnp.zeros((8, width), jnp.float32)
            halo[side] = zeros
            wetp[pl.ds((0, PAD + rows)[side], PAD), :] = zeros
            ha[pl.ds((0, PAD + rows)[side], PAD), :] = zeros

    def wait_halo(side):
        @pl.when(present[side])
        def _():
            halo_copy(1 - side).wait_recv()

    def flux(k):
        slot = lax.rem(k, SLOTS)
        after = lax.rem(k + 1, SLOTS)

        @pl.when(k + SLOTS - 1 < n)
        def _():
            for copy in ring(k + SLOTS - 1):
                copy.start()

        @pl.when(k == 0)
        def _():
            for copy in ring(k):
                copy.wait()
            wait_halo(0)
            prv[...] = halo[0]

        @pl.when(k < n - 1)
        def _():
            for copy in ring(k + 1):
                copy.wait()
            thick = ((surf[ds(k + 1, 8), :] - bed[ds(k + 1, 8), :]) / layers)[:1]
            for m in range(lh):
                c = cs[after, m, 0:1, :]
                u = us[after, m].astype(jnp.float32)[:1]
                nxt[m:m + 1, :] = c
                nxt[lh + m:lh + m + 1, :] = u
                nxt[2 * lh + m:2 * lh + m + 1, :] = u * c * thick

        @pl.when(k == n - 1)
        def _():
            wait_halo(1)
            nxt[...] = halo[1]

        @pl.when((k > 0) & (k < n - 1))
        def _():
            wetp[ds(k, CH, PAD), :] = ws[slot].astype(jnp.float32)

        @pl.when(k == 0)
        def _():
            wetp[PAD + 8:PAD + CH, :] = ws[slot, 8:, :].astype(jnp.float32)

        @pl.when(k == n - 1)
        def _():
            wetp[PAD + rows - CH:PAD + rows - 8, :] = ws[slot, :8, :].astype(jnp.float32)

        depth = surf[ds(k), :] - bed[ds(k), :]
        thick = depth / layers
        settle = sett[ds(k), :]
        erode = es[slot]
        inverse = layers / depth
        total = None
        col = lax.broadcasted_iota(jnp.int32, (CH, width), 1)
        for m in range(lh):
            c = cs[slot, m]
            u = us[slot, m].astype(jnp.float32)
            v = vs[slot, m].astype(jnp.float32)
            q = u * c * thick
            cn, un, qn = nxt[m:m + 1, :], nxt[lh + m:lh + m + 1, :], nxt[2 * lh + m:2 * lh + m + 1, :]
            cp, up, qp = prv[m:m + 1, :], prv[lh + m:lh + m + 1, :], prv[2 * lh + m:2 * lh + m + 1, :]
            low = face(down_rows(u, up), u, down_rows(c, cp), c)
            high = up_rows(low, face(u[CH - 1:], un, c[CH - 1:], cn))
            left = face(from_left(v), v, from_left(c), c)
            right = jnp.where(
                col == width - 1, jnp.maximum(0.5 * v, 0.0) * c, pltpu.roll(left, width - 1, 1)
            )
            advect = high - low + right - left
            fall = -settle * c
            if m < lh - 1:
                source = settle * cs[slot, m + 1] + fall
            else:
                source = fall
            if m == 0:
                source = source + bottom * erode
            out[m, ds(k), :] = c - ADVECT_RATE * advect + inverse * source
            p = v * c * thick
            spread = 0.5 * (up_rows(q, qn) - down_rows(q, qp) + from_right(p) - from_left(p))
            term = FLUX_GAIN * spread
            if m == 0:
                term = term + bottom * (fall + erode)
            total = term if total is None else total + term
            prv[m:m + 1, :] = c[CH - 1:]
            prv[lh + m:lh + m + 1, :] = u[CH - 1:]
            prv[2 * lh + m:2 * lh + m + 1, :] = q[CH - 1:]
        ha[ds(k, CH, PAD), :] = total

    def tick(t, _):
        @pl.when((t < ahead) & (t > 0))
        def _():
            start_conc(t)

        @pl.when(t < n)
        def _():
            flux(t)

        kd = t - ahead
        ku = t - l - LAG

        @pl.when((kd >= 0) & (kd < n))
        def _():
            @pl.when(has_up)
            def _():
                sum_down(kd).wait_recv()
                dbuf[ds(kd), :] += ha[ds(kd, CH, PAD), :]

            @pl.when(jnp.logical_not(has_up))
            def _():
                dbuf[ds(kd), :] = ha[ds(kd, CH, PAD), :]

            @pl.when(has_dn)
            def _():
                sum_down(kd).start()

            @pl.when(lax.rem(kd, 2) == 1)
            def _():
                start_conc(jnp.maximum(ahead, 1) + lax.div(kd, 2))

        @pl.when(kd == n - 1)
        def _():
            def rest(k, _):
                start_conc(k)
                return 0

            lax.fori_loop(jnp.maximum(ahead, 1) + n // 2, n, rest, 0)

        @pl.when((ku >= 0) & (ku < n))
        def _():
            @pl.when(has_dn)
            def _():
                sum_up(ku).wait_recv()
                ubuf[ds(ku), :] += ha[ds(ku, CH, PAD), :]

            @pl.when(jnp.logical_not(has_dn))
            def _():
                ubuf[ds(ku), :] = ha[ds(ku, CH, PAD), :]

            @pl.when(has_up)
            def _():
                sum_up(ku).start()

        return 0

    lax.fori_loop(0, n + nl - 1 + LAG, tick, 0)

    def first_height(k, _):
        total = dbuf[ds(k), :] + ubuf[ds(k), :] - ha[ds(k, CH, PAD), :]
        ha[ds(k, CH, PAD), :] = bed[ds(k), :] - POROSITY_GAIN * wetp[ds(k, CH, PAD), :] * total
        return 0

    lax.fori_loop(0, n, first_height, 0)
    for side in range(2):
        @pl.when(present[side])
        def _():
            height_copy(side).start()
    for side in range(2):
        @pl.when(present[side])
        def _():
            height_copy(1 - side).wait_recv()
            wet_copy(1 - side).wait_recv()
            height_copy(side).wait_send()

    def slide(src, dst, first, last, shift):
        def block(i, _):
            here = pl.ds(pl.multiple_of(i * 8, 8), 8)
            low = jnp.maximum(i * 8 - 1, 0)
            high = jnp.minimum(i * 8 + 8, rows + 2 * PAD - 1)
            h, w = src[here, :], wetp[here, :]
            hp, wp = src[pl.ds(low, 1), :], wetp[pl.ds(low, 1), :]
            hn, wn = src[pl.ds(high, 1), :], wetp[pl.ds(high, 1), :]
            ml = move(down_rows(h, hp) - h, down_rows(w, wp), w)
            mh = up_rows(ml, move(h[7:] - hn, w[7:], wn))
            yl = move(from_left(h) - h, from_left(w), w)
            yr = pltpu.roll(yl, width - 1, 1)
            dst[pl.ds(pl.multiple_of(i * 8 - shift, 8), 8), :] = h - mh + ml - yr + yl
            return 0

        lax.fori_loop(first, last, block, 0)

    blocks = (rows + 2 * PAD) // 8
    src, dst = ha, hb
    for sweep in range(SWEEPS - 1):
        slide(src, dst, 0, blocks, 0)
        src, dst = dst, src
    slide(src, out_h, 1, blocks - 1, PAD)

    def sent(k, _):
        @pl.when(has_dn)
        def _():
            sum_down(k).wait_send()

        return 0

    lax.fori_loop(0, n, sent, 0)

    def scale(k, _):
        depth = surf[ds(k), :] - bed[ds(k), :]
        new_depth = jnp.maximum(surf[ds(k), :] - out_h[ds(k), :], DEPTH_FLOOR)
        ratio = depth / new_depth
        for m in range(lh):
            out[m, ds(k), :] = out[m, ds(k), :] * ratio
        dbuf[ds(k), :] = layers * sett[ds(k), :] / new_depth
        return 0

    lax.fori_loop(0, n, scale, 0)

    def finish(k, _):
        @pl.when(has_up)
        def _():
            conc_down(k).wait_recv()
            out[lh - 1, ds(k), :] = out[lh - 1, ds(k), :] + dbuf[ds(k), :] * cup[ds(k), :]
            sum_up(k).wait_send()

        @pl.when(has_dn)
        def _():
            conc_down(k).wait_send()

        return 0

    lax.fori_loop(0, n, finish, 0)
    for side in range(2):
        @pl.when(present[side])
        def _():
            halo_copy(side).wait_send()
            wet_copy(side).wait_send()


def body(
    concentration, east_velocity, north_velocity, settling, surface, bed_level, erosion, wet_mask
):
    lh, rows, width = concentration.shape
    nb, nl = lax.axis_size("bed"), lax.axis_size("layer")
    n = rows // CH
    f32, bf16 = jnp.float32, jnp.bfloat16
    tall = rows + 2 * PAD
    vmem = pltpu.VMEM
    dma = pltpu.SemaphoreType.DMA
    cells = lh * rows * width
    return pl.pallas_call(
        functools.partial(kernel, nb, nl),
        out_shape=(
            jax.ShapeDtypeStruct((lh, rows, width), f32),
            jax.ShapeDtypeStruct((rows, width), f32),
        ),
        in_specs=[pl.BlockSpec(memory_space=pl.ANY)] * 8,
        out_specs=[pl.BlockSpec(memory_space=pltpu.VMEM)] * 2,
        scratch_shapes=[
            vmem((SLOTS, lh, CH, width), f32),
            vmem((SLOTS, lh, CH, width), bf16),
            vmem((SLOTS, lh, CH, width), bf16),
            vmem((SLOTS, CH, width), f32),
            vmem((SLOTS, CH, width), jnp.int32),
            vmem((2, lh, 8, width), f32),
            vmem((2, lh, 16, width), bf16),
            vmem((2, 8, width), jnp.int32),
            vmem((rows, width), f32),
            vmem((rows, width), f32),
            vmem((rows, width), f32),
            vmem((tall, width), f32),
            vmem((tall, width), f32),
            vmem((tall, width), f32),
            vmem((rows, width), f32),
            vmem((rows, width), f32),
            vmem((rows, width), f32),
            vmem((2, 8, width), f32),
            vmem((2, 8, width), f32),
            vmem((8, width), f32),
            vmem((8, width), f32),
            dma((SLOTS, 5)),
            dma((2, 3)),
            dma((3,)),
            dma((2,)), dma((2,)),
            dma((2,)), dma((2,)),
            dma((2,)), dma((2,)),
            dma((n,)), dma((n,)),
            dma((n,)), dma((n,)),
            dma((n,)), dma((n,)),
        ],
        compiler_params=pltpu.CompilerParams(
            collective_id=0, has_side_effects=True, vmem_limit_bytes=63 << 20
        ),
        cost_estimate=pl.CostEstimate(
            flops=100 * cells, bytes_accessed=24 * cells, transcendentals=0
        ),
    )(
        concentration, east_velocity, north_velocity, settling, surface, bed_level, erosion,
        wet_mask,
    )


def solution(mesh):
    layered = P("layer", "bed", None)
    flat = P("bed", None)
    return jax.shard_map(
        body, mesh=mesh, in_specs=(layered,) * 3 + (flat,) * 5, out_specs=(layered, flat),
        check_vma=False,
    )
```

```python
import functools

import jax
import jax.numpy as jnp
from jax import lax
from jax.experimental import pallas as pl
from jax.experimental.pallas import tpu as pltpu
from jax.sharding import PartitionSpec as P

SWEEPS = 4
ADVECT_RATE = 0.1
FLUX_GAIN = 0.15
POROSITY_GAIN = 1.0 / 0.6
RELAX_RATE = 0.2
CRIT_SLOPE = 0.5
DEPTH_FLOOR = 1.0

CH = 16
PAD = 8
SLOTS = 4
CD = 8
LEAD, LEAD_HOP = 1, 1
EVERY = 99
HOP = 2
LAG = 0
MESH = pl.DeviceIdType.MESH


def down_rows(x, first):
    row = lax.broadcasted_iota(jnp.int32, x.shape, 0)
    return jnp.where(row == 0, first, pltpu.roll(x, 1, 0))


def up_rows(x, last):
    n = x.shape[0]
    row = lax.broadcasted_iota(jnp.int32, x.shape, 0)
    return jnp.where(row == n - 1, last, pltpu.roll(x, n - 1, 0))


def from_left(x):
    col = lax.broadcasted_iota(jnp.int32, x.shape, 1)
    return jnp.where(col == 0, 0.0, pltpu.roll(x, 1, 1))


def from_right(x):
    w = x.shape[1]
    col = lax.broadcasted_iota(jnp.int32, x.shape, 1)
    return jnp.where(col == w - 1, 0.0, pltpu.roll(x, w - 1, 1))


def face(speed_a, speed_b, val_a, val_b):
    f = 0.5 * (speed_a + speed_b)
    return jnp.maximum(f, 0.0) * val_a + jnp.minimum(f, 0.0) * val_b


def move(drop, weight):
    return (drop - jnp.clip(drop, -CRIT_SLOPE, CRIT_SLOPE)) * weight


def kernel(
    nb, nl, c_hbm, u_hbm, v_hbm, sett_hbm, surf_hbm, bed_hbm, eros_hbm, wet_hbm,
    out_hbm, out_h_hbm,
    out, out_h, wx, wy, cs, us, vs, es, ws, ce, ue, we, sett, surf, bed, wetp, ha, hb, dbuf, ubuf, cup,
    edge_out, halo, prv, nxt,
    ring_sem, edge_sem, full_sem, halo_ss, halo_rs, wet_ss, wet_rs, h_ss, h_rs,
    d_ss, d_rs, u_ss, u_rs, c_ss, c_rs, out_sem, early_sem,
):
    lh, rows, width = c_hbm.shape
    n = rows // CH
    nd = rows // CD
    per = CH // CD
    layers = lh * nl
    l = lax.axis_index("layer")
    b = lax.axis_index("bed")
    has_dn, has_up = l > 0, l < nl - 1
    has_lo, has_hi = b > 0, b < nb - 1
    bottom = (l == 0).astype(jnp.float32)
    neighbours = (
        (has_lo, (b - 1, l)), (has_hi, (b + 1, l)), (has_dn, (b, l - 1)), (has_up, (b, l + 1)),
    )

    def ds(k, size=CH, off=0):
        return pl.ds(pl.multiple_of(k * CH + off, 8), size)

    def dd(k, off=0):
        return pl.ds(pl.multiple_of(k * CD + off, 8), CD)

    edges = []
    for side, (start8, start16) in enumerate(((0, 0), (rows - 8, rows - 16))):
        edges.append((
            pltpu.make_async_copy(c_hbm.at[:, pl.ds(start8, 8)], ce.at[side], edge_sem.at[side, 0]),
            pltpu.make_async_copy(u_hbm.at[:, pl.ds(start16, 16)], ue.at[side], edge_sem.at[side, 1]),
            pltpu.make_async_copy(wet_hbm.at[pl.ds(start8, 8)], we.at[side], edge_sem.at[side, 2]),
        ))
    fulls = [
        pltpu.make_async_copy(src, dst, full_sem.at[i])
        for i, (src, dst) in enumerate(((surf_hbm, surf), (bed_hbm, bed), (sett_hbm, sett)))
    ]

    def ring(k):
        s = lax.rem(k, SLOTS)
        return (
            pltpu.make_async_copy(c_hbm.at[:, ds(k)], cs.at[s], ring_sem.at[s, 0]),
            pltpu.make_async_copy(u_hbm.at[:, ds(k)], us.at[s], ring_sem.at[s, 1]),
            pltpu.make_async_copy(v_hbm.at[:, ds(k)], vs.at[s], ring_sem.at[s, 2]),
            pltpu.make_async_copy(eros_hbm.at[ds(k)], es.at[s], ring_sem.at[s, 3]),
            pltpu.make_async_copy(wet_hbm.at[ds(k)], ws.at[s], ring_sem.at[s, 4]),
        )

    for group in edges:
        for copy in group:
            copy.start()
    for copy in fulls:
        copy.start()
    for k in range(min(SLOTS - 1, n)):
        for copy in ring(k):
            copy.start()

    def remote(src, dst, ss, rs, target):
        return pltpu.make_async_remote_copy(
            src_ref=src, dst_ref=dst, send_sem=ss, recv_sem=rs, device_id=target,
            device_id_type=MESH,
        )

    def halo_copy(side):
        return remote(
            edge_out.at[side], halo.at[1 - side], halo_ss.at[side], halo_rs.at[1 - side],
            (b - 1 + 2 * side, l),
        )

    pad_src = (PAD, rows)
    pad_dst = (PAD + rows, 0)

    def wet_copy(side):
        return remote(
            wetp.at[pl.ds(pad_src[side], PAD)], wetp.at[pl.ds(pad_dst[side], PAD)],
            wet_ss.at[side], wet_rs.at[1 - side], (b - 1 + 2 * side, l),
        )

    def height_copy(side):
        return remote(
            ha.at[pl.ds(pad_src[side], PAD)], ha.at[pl.ds(pad_dst[side], PAD)],
            h_ss.at[side], h_rs.at[1 - side], (b - 1 + 2 * side, l),
        )

    def sum_down(k):
        return remote(dbuf.at[dd(k)], dbuf.at[dd(k)], d_ss.at[k], d_rs.at[k], (b, l - 1))

    def sum_up(k):
        return remote(ubuf.at[dd(k)], ubuf.at[dd(k)], u_ss.at[k], u_rs.at[k], (b, l + 1))

    def conc_down(k):
        return remote(c_hbm.at[0, ds(k)], cup.at[ds(k)], c_ss.at[k], c_rs.at[k], (b, l - 1))

    present = (has_lo, has_hi)

    barrier = pltpu.get_barrier_semaphore()
    for there, target in neighbours:
        @pl.when(there)
        def _():
            pl.semaphore_signal(barrier, inc=1, device_id=target, device_id_type=MESH)
    pl.semaphore_wait(barrier, sum(there.astype(jnp.int32) for there, _ in neighbours))

    def start_conc(k):
        @pl.when(has_dn & (k < n))
        def _():
            conc_down(k).start()

    ahead = nl - 1 - l
    lead = jnp.minimum(LEAD + LEAD_HOP * ahead, n)

    def send_conc(first, last):
        def one(k, _):
            start_conc(k)
            return 0

        lax.fori_loop(first, last, one, 0)

    send_conc(0, lead)

    for copy in fulls:
        copy.wait()
    for side in range(2):
        for copy in edges[side]:
            copy.wait()
        row8, row16, row = ((0, 0, 0), (7, 15, rows - 1))[side]
        thick = (surf[row:row + 1, :] - bed[row:row + 1, :]) / layers
        for m in range(lh):
            c = ce[side, m, row8:row8 + 1, :]
            u = ue[side, m].astype(jnp.float32)[row16:row16 + 1, :]
            edge_out[side, m:m + 1, :] = c
            edge_out[side, lh + m:lh + m + 1, :] = u
            edge_out[side, 2 * lh + m:2 * lh + m + 1, :] = u * c * thick
        for row in range(3 * lh, 8):
            edge_out[side, row:row + 1, :] = jnp.zeros((1, width), jnp.float32)
        wetp[pl.ds(pad_src[side], PAD), :] = we[side].astype(jnp.float32)

        @pl.when(present[side])
        def _():
            halo_copy(side).start()
            wet_copy(side).start()

        @pl.when(jnp.logical_not(present[side]))
        def _():
            zeros = jnp.zeros((8, width), jnp.float32)
            halo[side] = zeros
            wetp[pl.ds((0, PAD + rows)[side], PAD), :] = zeros
            ha[pl.ds((0, PAD + rows)[side], PAD), :] = zeros

    def wait_halo(side):
        @pl.when(present[side])
        def _():
            halo_copy(1 - side).wait_recv()

    def flux(k):
        slot = lax.rem(k, SLOTS)
        after = lax.rem(k + 1, SLOTS)

        @pl.when(k + SLOTS - 1 < n)
        def _():
            for copy in ring(k + SLOTS - 1):
                copy.start()

        @pl.when(k == 0)
        def _():
            for copy in ring(k):
                copy.wait()
            wait_halo(0)
            prv[...] = halo[0]

        @pl.when(k < n - 1)
        def _():
            for copy in ring(k + 1):
                copy.wait()
            thick = ((surf[ds(k + 1, 8), :] - bed[ds(k + 1, 8), :]) / layers)[:1]
            for m in range(lh):
                c = cs[after, m, 0:1, :]
                u = us[after, m].astype(jnp.float32)[:1]
                nxt[m:m + 1, :] = c
                nxt[lh + m:lh + m + 1, :] = u
                nxt[2 * lh + m:2 * lh + m + 1, :] = u * c * thick

        @pl.when(k == n - 1)
        def _():
            wait_halo(1)
            nxt[...] = halo[1]

        @pl.when((k > 0) & (k < n - 1))
        def _():
            wetp[ds(k, CH, PAD), :] = ws[slot].astype(jnp.float32)

        @pl.when(k == 0)
        def _():
            wetp[PAD + 8:PAD + CH, :] = ws[slot, 8:, :].astype(jnp.float32)

        @pl.when(k == n - 1)
        def _():
            wetp[PAD + rows - CH:PAD + rows - 8, :] = ws[slot, :8, :].astype(jnp.float32)

        depth = surf[ds(k), :] - bed[ds(k), :]
        thick = depth / layers
        settle = sett[ds(k), :]
        erode = es[slot]
        inverse = layers / depth
        total = None
        col = lax.broadcasted_iota(jnp.int32, (CH, width), 1)
        for m in range(lh):
            c = cs[slot, m]
            u = us[slot, m].astype(jnp.float32)
            v = vs[slot, m].astype(jnp.float32)
            q = u * c * thick
            cn, un, qn = nxt[m:m + 1, :], nxt[lh + m:lh + m + 1, :], nxt[2 * lh + m:2 * lh + m + 1, :]
            cp, up, qp = prv[m:m + 1, :], prv[lh + m:lh + m + 1, :], prv[2 * lh + m:2 * lh + m + 1, :]
            low = face(down_rows(u, up), u, down_rows(c, cp), c)
            high = up_rows(low, face(u[CH - 1:], un, c[CH - 1:], cn))
            left = face(from_left(v), v, from_left(c), c)
            right = jnp.where(
                col == width - 1, jnp.maximum(0.5 * v, 0.0) * c, pltpu.roll(left, width - 1, 1)
            )
            advect = high - low + right - left
            fall = -settle * c
            if m < lh - 1:
                source = settle * cs[slot, m + 1] + fall
            else:
                source = fall
            if m == 0:
                source = source + bottom * erode
            out[m, ds(k), :] = c - ADVECT_RATE * advect + inverse * source
            p = v * c * thick
            spread = 0.5 * (up_rows(q, qn) - down_rows(q, qp) + from_right(p) - from_left(p))
            term = FLUX_GAIN * spread
            if m == 0:
                term = term + bottom * (fall + erode)
            total = term if total is None else total + term
            prv[m:m + 1, :] = c[CH - 1:]
            prv[lh + m:lh + m + 1, :] = u[CH - 1:]
            prv[2 * lh + m:2 * lh + m + 1, :] = q[CH - 1:]
        ha[ds(k, CH, PAD), :] = total

    def weigh(i):
        here = pl.ds(pl.multiple_of(i * 8, 8), 8)
        w = wetp[here, :]
        wx[here, :] = RELAX_RATE * w * down_rows(w, wetp[pl.ds(jnp.maximum(i * 8 - 1, 0), 1), :])
        wy[here, :] = RELAX_RATE * w * from_left(w)

    def tick(t, _):
        @pl.when((t < nd) & (lax.rem(t, per) == 0))
        def _():
            flux(lax.div(t, per))

        kd = t - HOP * ahead
        ku = t - HOP * l - LAG

        @pl.when((kd >= 0) & (kd < nd))
        def _():
            @pl.when(has_up)
            def _():
                sum_down(kd).wait_recv()
                dbuf[dd(kd), :] += ha[dd(kd, PAD), :]

            @pl.when(jnp.logical_not(has_up))
            def _():
                dbuf[dd(kd), :] = ha[dd(kd, PAD), :]

            @pl.when(has_dn)
            def _():
                sum_down(kd).start()

            @pl.when(lax.rem(kd, EVERY) == EVERY - 1)
            def _():
                start_conc(lead + lax.div(kd, EVERY))

        @pl.when(kd == nd - 1)
        def _():
            send_conc(lead + nd // EVERY, n)

        @pl.when((ku >= 0) & (ku < nd))
        def _():
            @pl.when(has_dn)
            def _():
                sum_up(ku).wait_recv()
                ubuf[dd(ku), :] += ha[dd(ku, PAD), :]

            @pl.when(jnp.logical_not(has_dn))
            def _():
                ubuf[dd(ku), :] = ha[dd(ku, PAD), :]

            @pl.when(has_up)
            def _():
                sum_up(ku).start()

        @pl.when((t >= 2) & (t <= rows // 8))
        def _():
            weigh(t)

        return 0

    lax.fori_loop(0, nd + HOP * (nl - 1) + LAG, tick, 0)

    for side in range(2):
        @pl.when(present[side])
        def _():
            wet_copy(1 - side).wait_recv()
    for i in (0, 1, rows // 8 + 1):
        weigh(jnp.int32(i))

    def first_height(k, _):
        total = dbuf[ds(k), :] + ubuf[ds(k), :] - ha[ds(k, CH, PAD), :]
        ha[ds(k, CH, PAD), :] = bed[ds(k), :] - POROSITY_GAIN * wetp[ds(k, CH, PAD), :] * total
        return 0

    lax.fori_loop(0, n, first_height, 0)
    for side in range(2):
        @pl.when(present[side])
        def _():
            height_copy(side).start()
    for side in range(2):
        @pl.when(present[side])
        def _():
            height_copy(1 - side).wait_recv()
            height_copy(side).wait_send()

    def slide(src, dst, first, last, shift):
        def block(i, _):
            here = pl.ds(pl.multiple_of(i * 8, 8), 8)
            low = jnp.maximum(i * 8 - 1, 0)
            high = jnp.minimum(i * 8 + 8, rows + 2 * PAD - 1)
            h, g = src[here, :], wx[here, :]
            hp, hn = src[pl.ds(low, 1), :], src[pl.ds(high, 1), :]
            ml = move(down_rows(h, hp) - h, g)
            mh = up_rows(ml, move(h[7:] - hn, wx[pl.ds(high, 1), :]))
            yl = move(pltpu.roll(h, 1, 1) - h, wy[here, :])
            yr = pltpu.roll(yl, width - 1, 1)
            dst[pl.ds(pl.multiple_of(i * 8 - shift, 8), 8), :] = h - mh + ml - yr + yl
            return 0

        lax.fori_loop(first, last, block, 0)

    blocks = (rows + 2 * PAD) // 8
    src, dst = ha, hb
    for sweep in range(SWEEPS - 1):
        slide(src, dst, 0, blocks, 0)
        src, dst = dst, src
    slide(src, out_h, 1, blocks - 1, PAD)

    early = [pltpu.make_async_copy(out_h, out_h_hbm, early_sem.at[0])]
    early[0].start()

    def sent(k, _):
        @pl.when(has_dn)
        def _():
            sum_down(k).wait_send()

        @pl.when(has_up)
        def _():
            sum_up(k).wait_send()

        return 0

    lax.fori_loop(0, nd, sent, 0)

    def scale(k, _):
        depth = surf[ds(k), :] - bed[ds(k), :]
        new_depth = jnp.maximum(surf[ds(k), :] - out_h[ds(k), :], DEPTH_FLOOR)
        ratio = depth / new_depth
        for m in range(lh):
            out[m, ds(k), :] = out[m, ds(k), :] * ratio
        dbuf[ds(k), :] = layers * sett[ds(k), :] / new_depth
        return 0

    lax.fori_loop(0, n, scale, 0)

    early += [
        pltpu.make_async_copy(out.at[m], out_hbm.at[m], early_sem.at[1 + m]) for m in range(lh - 1)
    ]
    for copy in early[1:]:
        copy.start()

    def last_copy(k):
        return pltpu.make_async_copy(
            out.at[lh - 1, ds(k)], out_hbm.at[lh - 1, ds(k)], out_sem.at[k]
        )

    def finish(k, _):
        @pl.when(has_up)
        def _():
            conc_down(k).wait_recv()
            out[lh - 1, ds(k), :] = out[lh - 1, ds(k), :] + dbuf[ds(k), :] * cup[ds(k), :]

        last_copy(k).start()

        @pl.when(has_dn)
        def _():
            conc_down(k).wait_send()

        return 0

    lax.fori_loop(0, n, finish, 0)
    for copy in early:
        copy.wait()

    def written(k, _):
        last_copy(k).wait()
        return 0

    lax.fori_loop(0, n, written, 0)
    for side in range(2):
        @pl.when(present[side])
        def _():
            halo_copy(side).wait_send()
            wet_copy(side).wait_send()


def place(conc, height, out, out_h, conc_held, height_held, in_sem, out_sem):
    lh, rows, _ = conc.shape
    moves = []
    for part in range(lh + 1):
        src, held, dst = (
            (conc.at[part], conc_held.at[part], out.at[part])
            if part < lh else (height, height_held, out_h)
        )
        for k in range(rows // CH):
            here = pl.ds(k * CH, CH)
            moves.append((
                pltpu.make_async_copy(src.at[here], held.at[here], in_sem.at[part, k]),
                pltpu.make_async_copy(held.at[here], dst.at[here], out_sem.at[part, k]),
            ))
    for fetch, _ in moves:
        fetch.start()
    for fetch, store in moves:
        fetch.wait()
        store.start()
    for _, store in moves:
        store.wait()


def body(
    concentration, east_velocity, north_velocity, settling, surface, bed_level, erosion, wet_mask
):
    lh, rows, width = concentration.shape
    nb, nl = lax.axis_size("bed"), lax.axis_size("layer")
    n, nd = rows // CH, rows // CD
    f32, bf16 = jnp.float32, jnp.bfloat16
    tall = rows + 2 * PAD
    vmem = pltpu.VMEM
    dma = pltpu.SemaphoreType.DMA
    cells = lh * rows * width
    results = pl.pallas_call(
        functools.partial(kernel, nb, nl),
        out_shape=(
            jax.ShapeDtypeStruct((lh, rows, width), f32),
            jax.ShapeDtypeStruct((rows, width), f32),
        ),
        in_specs=[pl.BlockSpec(memory_space=pl.ANY)] * 8,
        out_specs=[pl.BlockSpec(memory_space=pl.ANY)] * 2,
        scratch_shapes=[
            vmem((lh, rows, width), f32),
            vmem((rows, width), f32),
            vmem((tall, width), f32),
            vmem((tall, width), f32),
            vmem((SLOTS, lh, CH, width), f32),
            vmem((SLOTS, lh, CH, width), bf16),
            vmem((SLOTS, lh, CH, width), bf16),
            vmem((SLOTS, CH, width), f32),
            vmem((SLOTS, CH, width), jnp.int32),
            vmem((2, lh, 8, width), f32),
            vmem((2, lh, 16, width), bf16),
            vmem((2, 8, width), jnp.int32),
            vmem((rows, width), f32),
            vmem((rows, width), f32),
            vmem((rows, width), f32),
            vmem((tall, width), f32),
            vmem((tall, width), f32),
            vmem((tall, width), f32),
            vmem((rows, width), f32),
            vmem((rows, width), f32),
            vmem((rows, width), f32),
            vmem((2, 8, width), f32),
            vmem((2, 8, width), f32),
            vmem((8, width), f32),
            vmem((8, width), f32),
            dma((SLOTS, 5)),
            dma((2, 3)),
            dma((3,)),
            dma((2,)), dma((2,)),
            dma((2,)), dma((2,)),
            dma((2,)), dma((2,)),
            dma((nd,)), dma((nd,)),
            dma((nd,)), dma((nd,)),
            dma((n,)), dma((n,)),
            dma((n,)), dma((lh,)),
        ],
        compiler_params=pltpu.CompilerParams(
            collective_id=0, has_side_effects=True, vmem_limit_bytes=63 << 20
        ),
        cost_estimate=pl.CostEstimate(
            flops=100 * cells, bytes_accessed=24 * cells, transcendentals=0
        ),
    )(
        concentration, east_velocity, north_velocity, settling, surface, bed_level, erosion,
        wet_mask,
    )
    return pl.pallas_call(
        place,
        out_shape=tuple(jax.ShapeDtypeStruct(r.shape, r.dtype) for r in results),
        in_specs=[pl.BlockSpec(memory_space=pl.ANY)] * 2,
        out_specs=[pl.BlockSpec(memory_space=pl.ANY)] * 2,
        scratch_shapes=[
            vmem((lh, rows, width), f32),
            vmem((rows, width), f32),
            dma((lh + 1, n)),
            dma((lh + 1, n)),
        ],
        compiler_params=pltpu.CompilerParams(vmem_limit_bytes=63 << 20),
        cost_estimate=pl.CostEstimate(
            flops=0, bytes_accessed=8 * (cells + rows * width), transcendentals=0
        ),
    )(*results)


def solution(mesh):
    layered = P("layer", "bed", None)
    flat = P("bed", None)
    return jax.shard_map(
        body, mesh=mesh, in_specs=(layered,) * 3 + (flat,) * 5, out_specs=(layered, flat),
        check_vma=False,
    )
```

```python
import functools

import jax
import jax.numpy as jnp
from jax import lax
from jax.experimental import pallas as pl
from jax.experimental.pallas import tpu as pltpu
from jax.sharding import PartitionSpec as P

SWEEPS = 4
ADVECT_RATE = 0.1
FLUX_GAIN = 0.15
POROSITY_GAIN = 1.0 / 0.6
RELAX_RATE = 0.2
CRIT_SLOPE = 0.5
DEPTH_FLOOR = 1.0

CH = 16
PAD = 8
SLOTS = 4
CD = 8
LEAD, LEAD_HOP = 1, 1
EVERY = 99
HOP = 2
LAG = 0
MESH = pl.DeviceIdType.MESH


def down_rows(x, first):
    row = lax.broadcasted_iota(jnp.int32, x.shape, 0)
    return jnp.where(row == 0, first, pltpu.roll(x, 1, 0))


def up_rows(x, last):
    n = x.shape[0]
    row = lax.broadcasted_iota(jnp.int32, x.shape, 0)
    return jnp.where(row == n - 1, last, pltpu.roll(x, n - 1, 0))


def from_left(x):
    col = lax.broadcasted_iota(jnp.int32, x.shape, 1)
    return jnp.where(col == 0, 0.0, pltpu.roll(x, 1, 1))


def from_right(x):
    w = x.shape[1]
    col = lax.broadcasted_iota(jnp.int32, x.shape, 1)
    return jnp.where(col == w - 1, 0.0, pltpu.roll(x, w - 1, 1))


def face(speed_a, speed_b, val_a, val_b):
    f = 0.5 * (speed_a + speed_b)
    return jnp.maximum(f, 0.0) * val_a + jnp.minimum(f, 0.0) * val_b


def move(drop, weight):
    return (drop - jnp.clip(drop, -CRIT_SLOPE, CRIT_SLOPE)) * weight


def kernel(
    nb, nl, c_hbm, u_hbm, v_hbm, sett_hbm, surf_hbm, bed_hbm, eros_hbm, wet_hbm,
    out, out_h, wx, wy, cs, us, vs, es, ws, ce, ue, we, sett, surf, bed, wetp, ha, hb, dbuf, ubuf, cup,
    edge_out, halo, prv, nxt,
    ring_sem, edge_sem, full_sem, halo_ss, halo_rs, wet_ss, wet_rs, h_ss, h_rs,
    d_ss, d_rs, u_ss, u_rs, c_ss, c_rs,
):
    lh, rows, width = c_hbm.shape
    n = rows // CH
    nd = rows // CD
    per = CH // CD
    layers = lh * nl
    l = lax.axis_index("layer")
    b = lax.axis_index("bed")
    has_dn, has_up = l > 0, l < nl - 1
    has_lo, has_hi = b > 0, b < nb - 1
    bottom = (l == 0).astype(jnp.float32)
    neighbours = (
        (has_lo, (b - 1, l)), (has_hi, (b + 1, l)), (has_dn, (b, l - 1)), (has_up, (b, l + 1)),
    )

    def ds(k, size=CH, off=0):
        return pl.ds(pl.multiple_of(k * CH + off, 8), size)

    def dd(k, off=0):
        return pl.ds(pl.multiple_of(k * CD + off, 8), CD)

    edges = []
    for side, (start8, start16) in enumerate(((0, 0), (rows - 8, rows - 16))):
        edges.append((
            pltpu.make_async_copy(c_hbm.at[:, pl.ds(start8, 8)], ce.at[side], edge_sem.at[side, 0]),
            pltpu.make_async_copy(u_hbm.at[:, pl.ds(start16, 16)], ue.at[side], edge_sem.at[side, 1]),
            pltpu.make_async_copy(wet_hbm.at[pl.ds(start8, 8)], we.at[side], edge_sem.at[side, 2]),
        ))
    fulls = [
        pltpu.make_async_copy(src, dst, full_sem.at[i])
        for i, (src, dst) in enumerate(((surf_hbm, surf), (bed_hbm, bed), (sett_hbm, sett)))
    ]

    def ring(k):
        s = lax.rem(k, SLOTS)
        return (
            pltpu.make_async_copy(c_hbm.at[:, ds(k)], cs.at[s], ring_sem.at[s, 0]),
            pltpu.make_async_copy(u_hbm.at[:, ds(k)], us.at[s], ring_sem.at[s, 1]),
            pltpu.make_async_copy(v_hbm.at[:, ds(k)], vs.at[s], ring_sem.at[s, 2]),
            pltpu.make_async_copy(eros_hbm.at[ds(k)], es.at[s], ring_sem.at[s, 3]),
            pltpu.make_async_copy(wet_hbm.at[ds(k)], ws.at[s], ring_sem.at[s, 4]),
        )

    for group in edges:
        for copy in group:
            copy.start()
    for copy in fulls:
        copy.start()
    for k in range(min(SLOTS - 1, n)):
        for copy in ring(k):
            copy.start()

    def remote(src, dst, ss, rs, target):
        return pltpu.make_async_remote_copy(
            src_ref=src, dst_ref=dst, send_sem=ss, recv_sem=rs, device_id=target,
            device_id_type=MESH,
        )

    def halo_copy(side):
        return remote(
            edge_out.at[side], halo.at[1 - side], halo_ss.at[side], halo_rs.at[1 - side],
            (b - 1 + 2 * side, l),
        )

    pad_src = (PAD, rows)
    pad_dst = (PAD + rows, 0)

    def wet_copy(side):
        return remote(
            wetp.at[pl.ds(pad_src[side], PAD)], wetp.at[pl.ds(pad_dst[side], PAD)],
            wet_ss.at[side], wet_rs.at[1 - side], (b - 1 + 2 * side, l),
        )

    def height_copy(side):
        return remote(
            ha.at[pl.ds(pad_src[side], PAD)], ha.at[pl.ds(pad_dst[side], PAD)],
            h_ss.at[side], h_rs.at[1 - side], (b - 1 + 2 * side, l),
        )

    def sum_down(k):
        return remote(dbuf.at[dd(k)], dbuf.at[dd(k)], d_ss.at[k], d_rs.at[k], (b, l - 1))

    def sum_up(k):
        return remote(ubuf.at[dd(k)], ubuf.at[dd(k)], u_ss.at[k], u_rs.at[k], (b, l + 1))

    def conc_down(k):
        return remote(c_hbm.at[0, ds(k)], cup.at[ds(k)], c_ss.at[k], c_rs.at[k], (b, l - 1))

    present = (has_lo, has_hi)

    barrier = pltpu.get_barrier_semaphore()
    for there, target in neighbours:
        @pl.when(there)
        def _():
            pl.semaphore_signal(barrier, inc=1, device_id=target, device_id_type=MESH)
    pl.semaphore_wait(barrier, sum(there.astype(jnp.int32) for there, _ in neighbours))

    def start_conc(k):
        @pl.when(has_dn & (k < n))
        def _():
            conc_down(k).start()

    ahead = nl - 1 - l
    lead = jnp.minimum(LEAD + LEAD_HOP * ahead, n)

    def send_conc(first, last):
        def one(k, _):
            start_conc(k)
            return 0

        lax.fori_loop(first, last, one, 0)

    send_conc(0, lead)

    for copy in fulls:
        copy.wait()
    for side in range(2):
        for copy in edges[side]:
            copy.wait()
        row8, row16, row = ((0, 0, 0), (7, 15, rows - 1))[side]
        thick = (surf[row:row + 1, :] - bed[row:row + 1, :]) / layers
        for m in range(lh):
            c = ce[side, m, row8:row8 + 1, :]
            u = ue[side, m].astype(jnp.float32)[row16:row16 + 1, :]
            edge_out[side, m:m + 1, :] = c
            edge_out[side, lh + m:lh + m + 1, :] = u
            edge_out[side, 2 * lh + m:2 * lh + m + 1, :] = u * c * thick
        for row in range(3 * lh, 8):
            edge_out[side, row:row + 1, :] = jnp.zeros((1, width), jnp.float32)
        wetp[pl.ds(pad_src[side], PAD), :] = we[side].astype(jnp.float32)

        @pl.when(present[side])
        def _():
            halo_copy(side).start()
            wet_copy(side).start()

        @pl.when(jnp.logical_not(present[side]))
        def _():
            zeros = jnp.zeros((8, width), jnp.float32)
            halo[side] = zeros
            wetp[pl.ds((0, PAD + rows)[side], PAD), :] = zeros
            ha[pl.ds((0, PAD + rows)[side], PAD), :] = zeros

    def wait_halo(side):
        @pl.when(present[side])
        def _():
            halo_copy(1 - side).wait_recv()

    def flux(k):
        slot = lax.rem(k, SLOTS)
        after = lax.rem(k + 1, SLOTS)

        @pl.when(k + SLOTS - 1 < n)
        def _():
            for copy in ring(k + SLOTS - 1):
                copy.start()

        @pl.when(k == 0)
        def _():
            for copy in ring(k):
                copy.wait()
            wait_halo(0)
            prv[...] = halo[0]

        @pl.when(k < n - 1)
        def _():
            for copy in ring(k + 1):
                copy.wait()
            thick = ((surf[ds(k + 1, 8), :] - bed[ds(k + 1, 8), :]) / layers)[:1]
            for m in range(lh):
                c = cs[after, m, 0:1, :]
                u = us[after, m].astype(jnp.float32)[:1]
                nxt[m:m + 1, :] = c
                nxt[lh + m:lh + m + 1, :] = u
                nxt[2 * lh + m:2 * lh + m + 1, :] = u * c * thick

        @pl.when(k == n - 1)
        def _():
            wait_halo(1)
            nxt[...] = halo[1]

        @pl.when((k > 0) & (k < n - 1))
        def _():
            wetp[ds(k, CH, PAD), :] = ws[slot].astype(jnp.float32)

        @pl.when(k == 0)
        def _():
            wetp[PAD + 8:PAD + CH, :] = ws[slot, 8:, :].astype(jnp.float32)

        @pl.when(k == n - 1)
        def _():
            wetp[PAD + rows - CH:PAD + rows - 8, :] = ws[slot, :8, :].astype(jnp.float32)

        depth = surf[ds(k), :] - bed[ds(k), :]
        thick = depth / layers
        settle = sett[ds(k), :]
        erode = es[slot]
        inverse = layers / depth
        total = None
        col = lax.broadcasted_iota(jnp.int32, (CH, width), 1)
        for m in range(lh):
            c = cs[slot, m]
            u = us[slot, m].astype(jnp.float32)
            v = vs[slot, m].astype(jnp.float32)
            q = u * c * thick
            cn, un, qn = nxt[m:m + 1, :], nxt[lh + m:lh + m + 1, :], nxt[2 * lh + m:2 * lh + m + 1, :]
            cp, up, qp = prv[m:m + 1, :], prv[lh + m:lh + m + 1, :], prv[2 * lh + m:2 * lh + m + 1, :]
            low = face(down_rows(u, up), u, down_rows(c, cp), c)
            high = up_rows(low, face(u[CH - 1:], un, c[CH - 1:], cn))
            left = face(from_left(v), v, from_left(c), c)
            right = jnp.where(
                col == width - 1, jnp.maximum(0.5 * v, 0.0) * c, pltpu.roll(left, width - 1, 1)
            )
            advect = high - low + right - left
            fall = -settle * c
            if m < lh - 1:
                source = settle * cs[slot, m + 1] + fall
            else:
                source = fall
            if m == 0:
                source = source + bottom * erode
            out[m, ds(k), :] = c - ADVECT_RATE * advect + inverse * source
            p = v * c * thick
            spread = 0.5 * (up_rows(q, qn) - down_rows(q, qp) + from_right(p) - from_left(p))
            term = FLUX_GAIN * spread
            if m == 0:
                term = term + bottom * (fall + erode)
            total = term if total is None else total + term
            prv[m:m + 1, :] = c[CH - 1:]
            prv[lh + m:lh + m + 1, :] = u[CH - 1:]
            prv[2 * lh + m:2 * lh + m + 1, :] = q[CH - 1:]
        ha[ds(k, CH, PAD), :] = total

    def weigh(i):
        here = pl.ds(pl.multiple_of(i * 8, 8), 8)
        w = wetp[here, :]
        wx[here, :] = RELAX_RATE * w * down_rows(w, wetp[pl.ds(jnp.maximum(i * 8 - 1, 0), 1), :])
        wy[here, :] = RELAX_RATE * w * from_left(w)

    def tick(t, _):
        @pl.when((t < nd) & (lax.rem(t, per) == 0))
        def _():
            flux(lax.div(t, per))

        kd = t - HOP * ahead
        ku = t - HOP * l - LAG

        @pl.when((kd >= 0) & (kd < nd))
        def _():
            @pl.when(has_up)
            def _():
                sum_down(kd).wait_recv()
                dbuf[dd(kd), :] += ha[dd(kd, PAD), :]

            @pl.when(jnp.logical_not(has_up))
            def _():
                dbuf[dd(kd), :] = ha[dd(kd, PAD), :]

            @pl.when(has_dn)
            def _():
                sum_down(kd).start()

            @pl.when(lax.rem(kd, EVERY) == EVERY - 1)
            def _():
                start_conc(lead + lax.div(kd, EVERY))

        @pl.when(kd == nd - 1)
        def _():
            send_conc(lead + nd // EVERY, n)

        @pl.when((ku >= 0) & (ku < nd))
        def _():
            @pl.when(has_dn)
            def _():
                sum_up(ku).wait_recv()
                ubuf[dd(ku), :] += ha[dd(ku, PAD), :]

            @pl.when(jnp.logical_not(has_dn))
            def _():
                ubuf[dd(ku), :] = ha[dd(ku, PAD), :]

            @pl.when(has_up)
            def _():
                sum_up(ku).start()

        @pl.when((t >= 2) & (t <= rows // 8))
        def _():
            weigh(t)

        return 0

    lax.fori_loop(0, nd + HOP * (nl - 1) + LAG, tick, 0)

    for side in range(2):
        @pl.when(present[side])
        def _():
            wet_copy(1 - side).wait_recv()
    for i in (0, 1, rows // 8 + 1):
        weigh(jnp.int32(i))

    def first_height(k, _):
        total = dbuf[ds(k), :] + ubuf[ds(k), :] - ha[ds(k, CH, PAD), :]
        ha[ds(k, CH, PAD), :] = bed[ds(k), :] - POROSITY_GAIN * wetp[ds(k, CH, PAD), :] * total
        return 0

    lax.fori_loop(0, n, first_height, 0)
    for side in range(2):
        @pl.when(present[side])
        def _():
            height_copy(side).start()
    for side in range(2):
        @pl.when(present[side])
        def _():
            height_copy(1 - side).wait_recv()
            height_copy(side).wait_send()

    def slide(src, dst, first, last, shift):
        def block(i, _):
            here = pl.ds(pl.multiple_of(i * 8, 8), 8)
            low = jnp.maximum(i * 8 - 1, 0)
            high = jnp.minimum(i * 8 + 8, rows + 2 * PAD - 1)
            h, g = src[here, :], wx[here, :]
            hp, hn = src[pl.ds(low, 1), :], src[pl.ds(high, 1), :]
            ml = move(down_rows(h, hp) - h, g)
            mh = up_rows(ml, move(h[7:] - hn, wx[pl.ds(high, 1), :]))
            yl = move(pltpu.roll(h, 1, 1) - h, wy[here, :])
            yr = pltpu.roll(yl, width - 1, 1)
            dst[pl.ds(pl.multiple_of(i * 8 - shift, 8), 8), :] = h - mh + ml - yr + yl
            return 0

        lax.fori_loop(first, last, block, 0)

    blocks = (rows + 2 * PAD) // 8
    src, dst = ha, hb
    for sweep in range(SWEEPS - 1):
        slide(src, dst, 0, blocks, 0)
        src, dst = dst, src
    slide(src, out_h, 1, blocks - 1, PAD)

    def sent(k, _):
        @pl.when(has_dn)
        def _():
            sum_down(k).wait_send()

        @pl.when(has_up)
        def _():
            sum_up(k).wait_send()

        return 0

    lax.fori_loop(0, nd, sent, 0)

    def scale(k, _):
        depth = surf[ds(k), :] - bed[ds(k), :]
        new_depth = jnp.maximum(surf[ds(k), :] - out_h[ds(k), :], DEPTH_FLOOR)
        ratio = depth / new_depth
        for m in range(lh):
            out[m, ds(k), :] = out[m, ds(k), :] * ratio
        dbuf[ds(k), :] = layers * sett[ds(k), :] / new_depth
        return 0

    lax.fori_loop(0, n, scale, 0)

    def finish(k, _):
        @pl.when(has_up)
        def _():
            conc_down(k).wait_recv()
            out[lh - 1, ds(k), :] = out[lh - 1, ds(k), :] + dbuf[ds(k), :] * cup[ds(k), :]

        @pl.when(has_dn)
        def _():
            conc_down(k).wait_send()

        return 0

    lax.fori_loop(0, n, finish, 0)
    for side in range(2):
        @pl.when(present[side])
        def _():
            halo_copy(side).wait_send()
            wet_copy(side).wait_send()


def place(conc, height, out, out_h, sem):
    lh, rows, _ = conc.shape
    moves = []
    for part in range(lh + 1):
        src, dst = (conc.at[part], out.at[part]) if part < lh else (height, out_h)
        for k in range(rows // 32):
            here = pl.ds(k * 32, 32)
            moves.append(pltpu.make_async_copy(src.at[here], dst.at[here], sem.at[part, k]))
    for move_out in moves:
        move_out.start()
    for move_out in moves:
        move_out.wait()


def body(
    concentration, east_velocity, north_velocity, settling, surface, bed_level, erosion, wet_mask
):
    lh, rows, width = concentration.shape
    nb, nl = lax.axis_size("bed"), lax.axis_size("layer")
    n, nd = rows // CH, rows // CD
    f32, bf16 = jnp.float32, jnp.bfloat16
    tall = rows + 2 * PAD
    vmem = pltpu.VMEM
    dma = pltpu.SemaphoreType.DMA
    cells = lh * rows * width
    results = pl.pallas_call(
        functools.partial(kernel, nb, nl),
        out_shape=(vmem((lh, rows, width), f32), vmem((rows, width), f32)),
        in_specs=[pl.BlockSpec(memory_space=pltpu.HBM)] * 8,
        out_specs=[pl.BlockSpec(memory_space=pltpu.VMEM)] * 2,
        scratch_shapes=[
            vmem((tall, width), f32),
            vmem((tall, width), f32),
            vmem((SLOTS, lh, CH, width), f32),
            vmem((SLOTS, lh, CH, width), bf16),
            vmem((SLOTS, lh, CH, width), bf16),
            vmem((SLOTS, CH, width), f32),
            vmem((SLOTS, CH, width), jnp.int32),
            vmem((2, lh, 8, width), f32),
            vmem((2, lh, 16, width), bf16),
            vmem((2, 8, width), jnp.int32),
            vmem((rows, width), f32),
            vmem((rows, width), f32),
            vmem((rows, width), f32),
            vmem((tall, width), f32),
            vmem((tall, width), f32),
            vmem((tall, width), f32),
            vmem((rows, width), f32),
            vmem((rows, width), f32),
            vmem((rows, width), f32),
            vmem((2, 8, width), f32),
            vmem((2, 8, width), f32),
            vmem((8, width), f32),
            vmem((8, width), f32),
            dma((SLOTS, 5)),
            dma((2, 3)),
            dma((3,)),
            dma((2,)), dma((2,)),
            dma((2,)), dma((2,)),
            dma((2,)), dma((2,)),
            dma((nd,)), dma((nd,)),
            dma((nd,)), dma((nd,)),
            dma((n,)), dma((n,)),
        ],
        compiler_params=pltpu.CompilerParams(
            collective_id=0, has_side_effects=True, vmem_limit_bytes=50 << 20
        ),
        cost_estimate=pl.CostEstimate(
            flops=100 * cells, bytes_accessed=24 * cells, transcendentals=0
        ),
    )(
        concentration, east_velocity, north_velocity, settling, surface, bed_level, erosion,
        wet_mask,
    )
    return pl.pallas_call(
        place,
        out_shape=(
            jax.ShapeDtypeStruct((lh, rows, width), f32),
            jax.ShapeDtypeStruct((rows, width), f32),
        ),
        in_specs=[pl.BlockSpec(memory_space=pltpu.VMEM)] * 2,
        out_specs=[pl.BlockSpec(memory_space=pltpu.HBM)] * 2,
        scratch_shapes=[dma((lh + 1, rows // 32))],
        compiler_params=pltpu.CompilerParams(vmem_limit_bytes=16 << 20),
        cost_estimate=pl.CostEstimate(
            flops=0, bytes_accessed=8 * (cells + rows * width), transcendentals=0
        ),
    )(*results)


def solution(mesh):
    layered = P("layer", "bed", None)
    flat = P("bed", None)
    return jax.shard_map(
        body, mesh=mesh, in_specs=(layered,) * 3 + (flat,) * 5, out_specs=(layered, flat),
        check_vma=False,
    )
```
